256 devices in a mesh: row: 8 (over z), col: 32 (over y, x, core).
Axes of the slice: x: 4, y: 4, z: 8, core: 2. Of those that a mesh axis runs over, the one named last changes fastest.
Arguments:
- activations: bfloat16 [262144, 1280], P(('row', 'col')), may hold values from -50 to 50
- out_grads: bfloat16 [262144, 1280], P(('row', 'col')), may hold values from -0.046875 to 0.046875
- error_buffer: bfloat16 [327680, 1280], P(('row', 'col')), may hold values from -8 to 8
- start_q: float32 [8, 1280], replicated, may hold values from -6 to 6
Outputs:
- new_error: bfloat16 [327680, 1280], P(('row', 'col'))
- factor_q: float32 [8, 1280], replicated
The draws below stay inside these ranges and needn't reach their ends.
All inputs are finite; a program needn't handle non-finite values.
Results may differ from the reference program's by a relative error of at most 0.001.
Values sent between devices are 32-bit elements; how exact they have to be, the bound alone decides.
No kernel may reach another device: no remote copies, remote signals or barrier semaphores. Data moves between devices by JAX's collectives and lax.ppermute only.
A program may use at most 64 MiB of HBM per device.

```python
import math
import jax
import jax.numpy as jnp
from jax import lax

D = 1280
RANK = 8
TOK_DEV = 1024
TOKENS = 262144
N_ROW = 8
N_COL = 32


def draw_activations(key, part):
    key = jax.random.fold_in(key, 11)
    key_scale, key_base = jax.random.split(key, 2)
    scales = jnp.exp(jax.random.uniform(key_scale, (D,), jnp.float32, 0.0, math.log(10.0)))
    values = jnp.clip(jax.random.normal(key_base, (TOKENS, D), jnp.float32), -4.0, 4.0) * scales
    return values.astype(jnp.bfloat16)


def shared_part(key, factor):
    key_left, key_right, key_strength = jax.random.split(key, 3)
    left = jnp.clip(jax.random.normal(key_left, (RANK, D), jnp.float32), -4.0, 4.0)
    right = jnp.clip(jax.random.normal(key_right, (RANK, D), jnp.float32), -4.0, 4.0)
    strength = jnp.exp(jax.random.uniform(key_strength, (RANK,), jnp.float32, 0.0, math.log(3.0))) * factor
    total = jnp.zeros((D, D), jnp.float32)
    for index in range(RANK):
        total = total + (strength[index] * left[index])[:, None] * right[index][None, :]
    return total


def draw_error_buffer(key, part):
    key = jax.random.fold_in(key, 23)
    key_noise, key_shared = jax.random.split(key, 2)
    replicas = N_ROW * N_COL
    noise = jnp.clip(jax.random.normal(key_noise, (replicas, D, D), jnp.float32), -6.0, 6.0) * 0.7
    common = shared_part(key_shared, 0.046)
    values = jnp.clip(noise + common[None, :, :], -8.0, 8.0)
    return values.reshape(replicas * D, D).astype(jnp.bfloat16)


def level_of(stream_key, extent, shards, low, high):
    def one(axis_at, blocks):
        draws = jax.random.uniform(jax.random.fold_in(jax.random.fold_in(stream_key, 6), axis_at), (blocks,), jnp.float32, low / len(shards), high / len(shards))
        return jnp.repeat(jnp.exp(draws), extent[axis_at] // blocks).reshape((-1,) + (1,) * (len(extent) - axis_at - 1))

    factor_of = one(*shards[0])
    for cut in shards[1:]:
        factor_of = factor_of * one(*cut)
    return factor_of


def centred(rng, extent, deviation, bound, shards=(), dtype=jnp.bfloat16):
    array = jax.random.normal(rng, extent, jnp.float32) * deviation
    if len(shards) > 0:
        array = level_of(rng, extent, shards, -0.22, 0.18) * array
    return jnp.clip(array, min=-bound, max=bound).astype(dtype)


def setup_inputs(seed: int = 0) -> dict:
    key_list = jax.random.split(jax.random.key(seed), 5)
    return {
        "activations": draw_activations(jax.random.fold_in(key_list[4], 71), 0),
        "out_grads": centred(key_list[1], (TOKENS, D), (16 * TOK_DEV) ** -0.5, 0.046875, ((0, 256),)),
        "error_buffer": draw_error_buffer(jax.random.fold_in(key_list[4], 71), 0),
        "start_q": centred(key_list[3], (RANK, D), 1.0, 6.0, (), jnp.float32),
    }


def orthonormal(p_sum):
    highest = lax.Precision.HIGHEST
    done = []
    for index in range(RANK):
        vector = p_sum[index]
        for basis in done:
            vector = vector - jnp.dot(basis, vector, precision=highest) * basis
        vector = vector / jnp.sqrt(jnp.dot(vector, vector, precision=highest))
        done.append(vector)
    return jnp.stack(done)

def reference(activations, out_grads, error_buffer, start_q):
    highest = lax.Precision.HIGHEST
    replicas = N_ROW * N_COL
    acts_all = activations.reshape(replicas, TOK_DEV, D)
    grads_all = out_grads.reshape(replicas, TOK_DEV, D)
    errs_all = error_buffer.reshape(replicas, D, D)

    def p_term(carry, items):
        acts_one, grads_one, errs_one = items
        left = lax.dot_general(start_q, grads_one.astype(jnp.float32), (((1,), (1,)), ((), ())), precision=highest)
        term = jnp.dot(left, acts_one.astype(jnp.float32), precision=highest)
        term = term + lax.dot_general(start_q, errs_one.astype(jnp.float32), (((1,), (1,)), ((), ())), precision=highest)
        return (carry + term, None)
    p_sum, _ = lax.scan(p_term, jnp.zeros((RANK, D), jnp.float32), (acts_all, grads_all, errs_all))
    p_hat = orthonormal(p_sum)

    def q_term(carry, items):
        acts_one, grads_one, errs_one = items
        left = lax.dot_general(p_hat, acts_one.astype(jnp.float32), (((1,), (1,)), ((), ())), precision=highest)
        term = jnp.dot(left, grads_one.astype(jnp.float32), precision=highest)
        term = term + jnp.dot(p_hat, errs_one.astype(jnp.float32), precision=highest)
        return (carry + term, None)
    q_sum, _ = lax.scan(q_term, jnp.zeros((RANK, D), jnp.float32), (acts_all, grads_all, errs_all))
    factor_q = q_sum / jnp.float32(replicas)
    update = lax.dot_general(p_hat, factor_q, (((0,), (0,)), ((), ())), precision=highest)

    def residual(items):
        acts_one, grads_one, errs_one = items
        grad_one = lax.dot_general(acts_one, grads_one, (((0,), (0,)), ((), ())), preferred_element_type=jnp.float32)
        return (grad_one + errs_one.astype(jnp.float32) - update).astype(jnp.bfloat16)
    new_error = lax.map(residual, (acts_all, grads_all, errs_all)).reshape(replicas * D, D)
    return (new_error, factor_q)
```

```python
import functools

import jax
import jax.numpy as jnp
from jax import lax
from jax.experimental import pallas as pl
from jax.experimental.pallas import tpu as pltpu
from jax.sharding import PartitionSpec as P

F32, BF16 = jnp.float32, jnp.bfloat16
BLOCK = 256
VMEM = pl.BlockSpec(memory_space=pltpu.VMEM)
ANY = pl.BlockSpec(memory_space=pl.ANY)
HBM = pl.BlockSpec(memory_space=pltpu.HBM)
AXES = ("row", "col")
NT = (((1,), (1,)), ((), ()))
NN = (((1,), (0,)), ((), ()))
TN = (((0,), (0,)), ((), ()))


def params():
    return pltpu.CompilerParams(vmem_limit_bytes=16 * 1024 * 1024)


def in_hbm(x):
    return pltpu.with_memory_space_constraint(x, pltpu.HBM)


def in_vmem(x):
    return pltpu.with_memory_space_constraint(x, pltpu.VMEM)


def parts_of(x):
    high = x.astype(BF16).astype(F32)
    rest = x - high
    mid = rest.astype(BF16).astype(F32)
    low = (rest - mid).astype(BF16).astype(F32)
    return high, mid, low


def stacked(x):
    high, mid, low = parts_of(x)
    return jnp.concatenate([high, mid, low, jnp.zeros_like(x)], axis=0).astype(BF16)


def times(lhs, rhs, dims):
    out = lax.dot_general(lhs, rhs, dims, preferred_element_type=F32)
    return out[0:8] + (out[8:16] + out[16:24])


def p_kernel(q_hbm, a_hbm, g_hbm, e_hbm, p_ref, a_ref, g_ref, e_ref, q_ref, sems, *, cuts):
    tokens, width = a_ref.shape
    copies = [pltpu.make_async_copy(q_hbm, q_ref, sems.at[0])]
    for src, dst, n in ((g_hbm, g_ref, cuts[0]), (a_hbm, a_ref, cuts[1]), (e_hbm, e_ref, cuts[2])):
        size = src.shape[0] // n
        for i in range(n):
            rows = pl.ds(i * size, size)
            copies.append(pltpu.make_async_copy(src.at[rows], dst.at[rows], sems.at[len(copies)]))
    for copy in copies:
        copy.start()
    queue = iter(copies)
    next(queue).wait()
    q = stacked(q_ref[...])
    lefts = []
    size = tokens // cuts[0]
    for i in range(cuts[0]):
        next(queue).wait()
        lefts.append(times(q, g_ref[pl.ds(i * size, size), :], NT))
    left = stacked(jnp.concatenate(lefts, axis=1))
    size = tokens // cuts[1]
    total = None
    for i in range(cuts[1]):
        next(queue).wait()
        at = slice(i * size, (i + 1) * size)
        term = times(left[:, at], a_ref[at, :], NN)
        total = term if total is None else total + term
    size = width // cuts[2]
    for i in range(cuts[2]):
        next(queue).wait()
        at = slice(i * size, (i + 1) * size)
        p_ref[:, at] = total[:, at] + times(q, e_ref[at, :], NT)


def p_local(start_q, activations, out_grads, error_buffer, cuts=(2, 2, 2)):
    return pl.pallas_call(
        functools.partial(p_kernel, cuts=cuts),
        out_shape=(
            jax.ShapeDtypeStruct(start_q.shape, F32),
            pltpu.VMEM(activations.shape, BF16),
            pltpu.VMEM(out_grads.shape, BF16),
            pltpu.VMEM(error_buffer.shape, BF16),
        ),
        in_specs=[HBM, HBM, HBM, HBM],
        out_specs=(VMEM, VMEM, VMEM, VMEM),
        scratch_shapes=[pltpu.VMEM(start_q.shape, F32), pltpu.SemaphoreType.DMA((1 + sum(cuts),))],
        compiler_params=params(),
        name="p_local",
    )(in_hbm(start_q), in_hbm(activations), in_hbm(out_grads), in_hbm(error_buffer))


def merged_rows(i, a_ref, g_ref, e_ref):
    at = slice(i * BLOCK, (i + 1) * BLOCK)
    product = lax.dot_general(a_ref[:, at], g_ref[...], TN, preferred_element_type=F32)
    return product + e_ref[at, :].astype(F32)


def merged_block(i, a, g, e, after):
    def kernel(a_ref, g_ref, e_ref, after_ref, m_ref):
        del after_ref
        m_ref[...] = merged_rows(i, a_ref, g_ref, e_ref)

    return pl.pallas_call(
        kernel,
        out_shape=pltpu.VMEM((BLOCK, e.shape[1]), F32),
        in_specs=[VMEM, VMEM, VMEM, ANY],
        out_specs=VMEM,
        compiler_params=params(),
        cost_estimate=pl.CostEstimate(
            flops=2 * a.shape[0] * BLOCK * g.shape[1], bytes_accessed=0, transcendentals=0
        ),
        name="merged_block",
    )(a, g, e, after)


def orthonormal(rest):
    rows = lax.broadcasted_iota(jnp.int32, (rest.shape[0], 1), 0)
    hat = jnp.zeros_like(rest)
    for j in range(rest.shape[0]):
        row = rest[j : j + 1]
        dots = jnp.sum(row * rest, axis=1, keepdims=True)
        square = dots[j : j + 1]
        hat = jnp.where(rows == j, row / jnp.sqrt(square), hat)
        rest = rest - (dots / square) * row
    return hat


def q_kernel(p_ref, a_ref, g_ref, e_ref, q_ref, hat_ref, m_ref, *, block):
    if block is not None:
        m_ref[...] = merged_rows(block, a_ref, g_ref, e_ref)
    hat = orthonormal(p_ref[...])
    hat_ref[...] = hat
    stack = stacked(hat)
    left = stacked(times(stack, a_ref[...], NT))
    q_ref[...] = times(stack, e_ref[...], NN) + times(left, g_ref[...], NN)


def q_local(p_sum, a, g, e, block):
    return pl.pallas_call(
        functools.partial(q_kernel, block=block),
        out_shape=(
            jax.ShapeDtypeStruct(p_sum.shape, F32),
            pltpu.VMEM(p_sum.shape, F32),
            pltpu.VMEM((BLOCK, e.shape[1]), F32),
        ),
        in_specs=[VMEM, VMEM, VMEM, VMEM],
        out_specs=(VMEM, VMEM, VMEM),
        compiler_params=params(),
        name="q_local",
    )(p_sum, a, g, e)


def update_kernel(total_ref, hat_ref, *refs, replicas, n):
    m_refs = refs[:n]
    out_hbm, f_hbm, f_ref, out_ref, sems = refs[n:]
    factor = total_ref[...] * (1.0 / replicas)
    f_ref[...] = factor
    copies = [pltpu.make_async_copy(f_ref, f_hbm, sems.at[n])]
    copies[0].start()
    p1, p2, p3 = parts_of(hat_ref[...])
    f1, f2, f3 = parts_of(factor)
    zero = jnp.zeros_like(p1)
    lhs = jnp.concatenate([p1, p1, p2, p2, p1, p3, zero, zero], axis=0).astype(BF16)
    rhs = jnp.concatenate([f1, f2, f1, f2, f3, f1, zero, zero], axis=0).astype(BF16)
    for i in range(n):
        at = slice(i * BLOCK, (i + 1) * BLOCK)
        update = lax.dot_general(lhs[:, at], rhs, TN, preferred_element_type=F32)
        out_ref[at, :] = (m_refs[i][...] - update).astype(BF16)
        copies.append(pltpu.make_async_copy(out_ref.at[at], out_hbm.at[at], sems.at[i]))
        copies[-1].start()
    for copy in copies:
        copy.wait()


def update(q_total, hat, blocks, replicas):
    n = len(blocks)
    shape = (n * BLOCK, q_total.shape[1])
    return pl.pallas_call(
        functools.partial(update_kernel, replicas=replicas, n=n),
        out_shape=(
            jax.ShapeDtypeStruct(shape, BF16),
            jax.ShapeDtypeStruct(q_total.shape, F32),
        ),
        in_specs=[VMEM] * (2 + n),
        out_specs=(HBM, HBM),
        scratch_shapes=[
            pltpu.VMEM(q_total.shape, F32),
            pltpu.VMEM(shape, BF16),
            pltpu.SemaphoreType.DMA((n + 1,)),
        ],
        compiler_params=params(),
        name="update",
    )(q_total, hat, *blocks)


CORES = 2


def permute(x, target):
    n_row, n_col = lax.axis_size("row"), lax.axis_size("col")
    pairs = []
    for i in range(n_row * n_col):
        row, col = target(*divmod(i, n_col))
        pairs.append((i, (row % n_row) * n_col + col))
    return lax.ppermute(x, AXES, pairs)


def gather_sum(x, groups):
    n = len(groups[0])
    every = jnp.broadcast_to(x[None], (n,) + x.shape)
    every = lax.all_to_all(every, AXES, 0, 0, axis_index_groups=groups, tiled=True)
    terms = [every[i] for i in range(n)]
    while len(terms) > 1:
        terms = [low + high for low, high in zip(terms[0::2], terms[1::2])]
    return terms[0]


def core_scatter(x, core, beside):
    half = x.shape[0] // CORES
    low, high = x[:half], x[half:]
    sent = jnp.where(core == 0, high, low)
    other, extra = lax.optimization_barrier((permute(sent, lambda r, c: (r, c ^ 1)), beside(sent)))
    return jnp.where(core == 0, low, high) + other, extra


def core_gather(x, core, beside):
    other, extra = lax.optimization_barrier((permute(x, lambda r, c: (r, c ^ 1)), beside(x)))
    rows = [jnp.where(core == 0, x, other), jnp.where(core == 0, other, x)]
    return jnp.concatenate(rows, axis=0), extra


def xy_groups():
    n_row, n_col = lax.axis_size("row"), lax.axis_size("col")
    return [
        [r * n_col + i * CORES + k for i in range(n_col // CORES)]
        for r in range(n_row)
        for k in range(CORES)
    ]


def z_groups():
    n_row, n_col = lax.axis_size("row"), lax.axis_size("col")
    return [[r * n_col + c for r in range(n_row)] for c in range(n_col)]


def on_device(activations, out_grads, error_buffer, start_q):
    replicas = lax.axis_size("row") * lax.axis_size("col")
    core = lax.axis_index("col") % CORES
    p, a, g, e = p_local(start_q, activations, out_grads, error_buffer)
    block = lambda i: lambda after: merged_block(i, a, g, e, after)
    p, m0 = core_scatter(p, core, block(0))
    p = gather_sum(gather_sum(p, xy_groups()), z_groups())
    p_sum, m1 = core_gather(p, core, block(1))
    q, hat, m2 = q_local(p_sum, a, g, e, 2)
    q, m3 = core_scatter(q, core, block(3))
    q = gather_sum(gather_sum(q, xy_groups()), z_groups())
    q_total, m4 = core_gather(q, core, block(4))
    return update(q_total, hat, [m0, m1, m2, m3, m4], replicas)


def solution(mesh):
    return jax.shard_map(
        on_device,
        mesh=mesh,
        in_specs=(P(AXES, None), P(AXES, None), P(AXES, None), P()),
        out_specs=(P(AXES, None), P()),
        check_vma=False,
    )
```

```python
import functools

import jax
import jax.numpy as jnp
from jax import lax
from jax.experimental import pallas as pl
from jax.experimental.pallas import tpu as pltpu
from jax.sharding import PartitionSpec as P

F32, BF16 = jnp.float32, jnp.bfloat16
BLOCK = 256
VMEM = pl.BlockSpec(memory_space=pltpu.VMEM)
ANY = pl.BlockSpec(memory_space=pl.ANY)
HBM = pl.BlockSpec(memory_space=pltpu.HBM)
AXES = ("row", "col")
NT = (((1,), (1,)), ((), ()))
NN = (((1,), (0,)), ((), ()))
TN = (((0,), (0,)), ((), ()))


def params():
    return pltpu.CompilerParams(vmem_limit_bytes=16 * 1024 * 1024)


def in_hbm(x):
    return pltpu.with_memory_space_constraint(x, pltpu.HBM)


def in_vmem(x):
    return pltpu.with_memory_space_constraint(x, pltpu.VMEM)


def parts_of(x):
    high = x.astype(BF16).astype(F32)
    rest = x - high
    mid = rest.astype(BF16).astype(F32)
    low = (rest - mid).astype(BF16).astype(F32)
    return high, mid, low


def stacked(x):
    high, mid, low = parts_of(x)
    return jnp.concatenate([high, mid, low, jnp.zeros_like(x)], axis=0).astype(BF16)


def times(lhs, rhs, dims):
    out = lax.dot_general(lhs, rhs, dims, preferred_element_type=F32)
    return out[0:8] + (out[8:16] + out[16:24])


def p_kernel(q_hbm, a_hbm, g_hbm, e_hbm, p_ref, a_ref, g_ref, e_ref, q_ref, sems, *, cuts):
    tokens, width = a_ref.shape
    copies = [pltpu.make_async_copy(q_hbm, q_ref, sems.at[0])]
    for src, dst, n in ((g_hbm, g_ref, cuts[0]), (a_hbm, a_ref, cuts[1]), (e_hbm, e_ref, cuts[2])):
        size = src.shape[0] // n
        for i in range(n):
            rows = pl.ds(i * size, size)
            copies.append(pltpu.make_async_copy(src.at[rows], dst.at[rows], sems.at[len(copies)]))
    for copy in copies:
        copy.start()
    queue = iter(copies)
    next(queue).wait()
    q = stacked(q_ref[...])
    lefts = []
    size = tokens // cuts[0]
    for i in range(cuts[0]):
        next(queue).wait()
        lefts.append(times(q, g_ref[pl.ds(i * size, size), :], NT))
    left = stacked(jnp.concatenate(lefts, axis=1))
    size = tokens // cuts[1]
    total = None
    for i in range(cuts[1]):
        next(queue).wait()
        at = slice(i * size, (i + 1) * size)
        term = times(left[:, at], a_ref[at, :], NN)
        total = term if total is None else total + term
    size = width // cuts[2]
    for i in range(cuts[2]):
        next(queue).wait()
        at = slice(i * size, (i + 1) * size)
        p_ref[:, at] = total[:, at] + times(q, e_ref[at, :], NT)


def p_local(start_q, activations, out_grads, error_buffer, cuts=(2, 2, 2)):
    return pl.pallas_call(
        functools.partial(p_kernel, cuts=cuts),
        out_shape=(
            jax.ShapeDtypeStruct(start_q.shape, F32),
            pltpu.VMEM(activations.shape, BF16),
            pltpu.VMEM(out_grads.shape, BF16),
            pltpu.VMEM(error_buffer.shape, BF16),
        ),
        in_specs=[HBM, HBM, HBM, HBM],
        out_specs=(VMEM, VMEM, VMEM, VMEM),
        scratch_shapes=[pltpu.VMEM(start_q.shape, F32), pltpu.SemaphoreType.DMA((1 + sum(cuts),))],
        compiler_params=params(),
        name="p_local",
    )(in_hbm(start_q), in_hbm(activations), in_hbm(out_grads), in_hbm(error_buffer))


def merged_rows(i, a_ref, g_ref, e_ref):
    at = slice(i * BLOCK, (i + 1) * BLOCK)
    product = lax.dot_general(a_ref[:, at], g_ref[...], TN, preferred_element_type=F32)
    return product + e_ref[at, :].astype(F32)


def merged_block(i, a, g, e, after):
    def kernel(a_ref, g_ref, e_ref, after_ref, m_ref):
        del after_ref
        m_ref[...] = merged_rows(i, a_ref, g_ref, e_ref)

    return pl.pallas_call(
        kernel,
        out_shape=pltpu.VMEM((BLOCK, e.shape[1]), F32),
        in_specs=[VMEM, VMEM, VMEM, ANY],
        out_specs=VMEM,
        compiler_params=params(),
        cost_estimate=pl.CostEstimate(
            flops=2 * a.shape[0] * BLOCK * g.shape[1], bytes_accessed=0, transcendentals=0
        ),
        name="merged_block",
    )(a, g, e, after)


def orthonormal(rest):
    rows = lax.broadcasted_iota(jnp.int32, (rest.shape[0], 1), 0)
    hat = jnp.zeros_like(rest)
    for j in range(rest.shape[0]):
        row = rest[j : j + 1]
        dots = jnp.sum(row * rest, axis=1, keepdims=True)
        square = dots[j : j + 1]
        hat = jnp.where(rows == j, row / jnp.sqrt(square), hat)
        rest = rest - (dots / square) * row
    return hat


def q_kernel(p_ref, a_ref, g_ref, e_ref, q_ref, hat_ref, m_ref, *, block):
    if block is not None:
        m_ref[...] = merged_rows(block, a_ref, g_ref, e_ref)
    hat = orthonormal(p_ref[...])
    hat_ref[...] = hat
    stack = stacked(hat)
    left = stacked(times(stack, a_ref[...], NT))
    q_ref[...] = times(stack, e_ref[...], NN) + times(left, g_ref[...], NN)


def q_local(p_sum, a, g, e, block):
    return pl.pallas_call(
        functools.partial(q_kernel, block=block),
        out_shape=(
            jax.ShapeDtypeStruct(p_sum.shape, F32),
            pltpu.VMEM(p_sum.shape, F32),
            pltpu.VMEM((BLOCK, e.shape[1]), F32),
        ),
        in_specs=[VMEM, VMEM, VMEM, VMEM],
        out_specs=(VMEM, VMEM, VMEM),
        compiler_params=params(),
        name="q_local",
    )(p_sum, a, g, e)


def update_kernel(total_ref, hat_ref, *refs, replicas, n):
    m_refs = refs[:n]
    out_hbm, f_hbm, f_ref, out_ref, sems = refs[n:]
    factor = total_ref[...] * (1.0 / replicas)
    f_ref[...] = factor
    copies = [pltpu.make_async_copy(f_ref, f_hbm, sems.at[n])]
    copies[0].start()
    p1, p2, p3 = parts_of(hat_ref[...])
    f1, f2, f3 = parts_of(factor)
    zero = jnp.zeros_like(p1)
    lhs = jnp.concatenate([p1, p1, p2, p2, p1, p3, zero, zero], axis=0).astype(BF16)
    rhs = jnp.concatenate([f1, f2, f1, f2, f3, f1, zero, zero], axis=0).astype(BF16)
    for i in range(n):
        at = slice(i * BLOCK, (i + 1) * BLOCK)
        update = lax.dot_general(lhs[:, at], rhs, TN, preferred_element_type=F32)
        out_ref[at, :] = (m_refs[i][...] - update).astype(BF16)
        copies.append(pltpu.make_async_copy(out_ref.at[at], out_hbm.at[at], sems.at[i]))
        copies[-1].start()
    for copy in copies:
        copy.wait()


def update(q_total, hat, blocks, replicas):
    n = len(blocks)
    shape = (n * BLOCK, q_total.shape[1])
    return pl.pallas_call(
        functools.partial(update_kernel, replicas=replicas, n=n),
        out_shape=(
            jax.ShapeDtypeStruct(shape, BF16),
            jax.ShapeDtypeStruct(q_total.shape, F32),
        ),
        in_specs=[VMEM] * (2 + n),
        out_specs=(HBM, HBM),
        scratch_shapes=[
            pltpu.VMEM(q_total.shape, F32),
            pltpu.VMEM(shape, BF16),
            pltpu.SemaphoreType.DMA((n + 1,)),
        ],
        compiler_params=params(),
        name="update",
    )(q_total, hat, *blocks)


CORES = 2


def permute(x, target):
    n_row, n_col = lax.axis_size("row"), lax.axis_size("col")
    pairs = []
    for i in range(n_row * n_col):
        row, col = target(*divmod(i, n_col))
        pairs.append((i, (row % n_row) * n_col + col))
    return lax.ppermute(x, AXES, pairs)


def gather_sum(x, groups):
    n = len(groups[0])
    every = jnp.broadcast_to(x[None], (n,) + x.shape)
    every = lax.all_to_all(every, AXES, 0, 0, axis_index_groups=groups, tiled=True)
    terms = [every[i] for i in range(n)]
    while len(terms) > 1:
        terms = [low + high for low, high in zip(terms[0::2], terms[1::2])]
    return terms[0]


def core_scatter(x, core, beside):
    half = x.shape[0] // CORES
    low, high = x[:half], x[half:]
    sent = jnp.where(core == 0, high, low)
    other, extra = lax.optimization_barrier((permute(sent, lambda r, c: (r, c ^ 1)), beside(sent)))
    return jnp.where(core == 0, low, high) + other, extra


def core_gather(x, core, beside):
    other, extra = lax.optimization_barrier((permute(x, lambda r, c: (r, c ^ 1)), beside(x)))
    rows = [jnp.where(core == 0, x, other), jnp.where(core == 0, other, x)]
    return jnp.concatenate(rows, axis=0), extra


def xy_groups(step):
    n_row, n_col = lax.axis_size("row"), lax.axis_size("col")
    n = n_col // CORES
    return [
        [r * n_col + i * step % n * CORES + k for i in range(n)]
        for r in range(n_row)
        for k in range(CORES)
    ]


def z_groups(order):
    n_col = lax.axis_size("col")
    return [[r * n_col + c for r in order] for c in range(n_col)]


def on_device(activations, out_grads, error_buffer, start_q):
    replicas = lax.axis_size("row") * lax.axis_size("col")
    core = lax.axis_index("col") & (CORES - 1)
    p, a, g, e = p_local(start_q, activations, out_grads, error_buffer)
    block = lambda i: lambda after: merged_block(i, a, g, e, after)
    p, m0 = core_scatter(p, core, block(0))
    p = gather_sum(gather_sum(p, xy_groups(7)), z_groups([1, 2, 0, 7, 6, 3, 5, 4]))
    p_sum, m1 = core_gather(p, core, block(1))
    q, hat, m2 = q_local(p_sum, a, g, e, 2)
    q, m3 = core_scatter(q, core, block(3))
    q = gather_sum(gather_sum(q, xy_groups(1)), z_groups([1, 2, 0, 7, 6, 3, 5, 4]))
    q_total, m4 = core_gather(q, core, block(4))
    return update(q_total, hat, [m0, m1, m2, m3, m4], replicas)


def solution(mesh):
    return jax.shard_map(
        on_device,
        mesh=mesh,
        in_specs=(P(AXES, None), P(AXES, None), P(AXES, None), P()),
        out_specs=(P(AXES, None), P()),
        check_vma=False,
    )
```

```python
import functools
import math

import jax
import jax.numpy as jnp
from jax import lax
from jax.experimental import pallas as pl
from jax.experimental.pallas import tpu as pltpu
from jax.sharding import PartitionSpec as P

F32, BF16 = jnp.float32, jnp.bfloat16
BLOCK = 256
VMEM = pl.BlockSpec(memory_space=pltpu.VMEM)
ANY = pl.BlockSpec(memory_space=pl.ANY)
HBM = pl.BlockSpec(memory_space=pltpu.HBM)
AXES = ("row", "col")
NT = (((1,), (1,)), ((), ()))
NN = (((1,), (0,)), ((), ()))
TN = (((0,), (0,)), ((), ()))


def params():
    return pltpu.CompilerParams(vmem_limit_bytes=16 * 1024 * 1024)


def in_hbm(x):
    return pltpu.with_memory_space_constraint(x, pltpu.HBM)


def in_vmem(x):
    return pltpu.with_memory_space_constraint(x, pltpu.VMEM)


def parts_of(x):
    high = x.astype(BF16).astype(F32)
    rest = x - high
    mid = rest.astype(BF16).astype(F32)
    low = (rest - mid).astype(BF16).astype(F32)
    return high, mid, low


def stacked(x):
    high, mid, low = parts_of(x)
    return jnp.concatenate([high, mid, low, jnp.zeros_like(x)], axis=0).astype(BF16)


def times(lhs, rhs, dims):
    out = lax.dot_general(lhs, rhs, dims, preferred_element_type=F32)
    return out[0:8] + (out[8:16] + out[16:24])


def p_kernel(q_hbm, a_hbm, g_hbm, e_hbm, p_ref, a_ref, g_ref, e_ref, q_ref, sems, *, cuts):
    tokens, width = a_ref.shape
    copies = [pltpu.make_async_copy(q_hbm, q_ref, sems.at[0])]
    for src, dst, n in ((g_hbm, g_ref, cuts[0]), (a_hbm, a_ref, cuts[1]), (e_hbm, e_ref, cuts[2])):
        size = src.shape[0] // n
        for i in range(n):
            rows = pl.ds(i * size, size)
            copies.append(pltpu.make_async_copy(src.at[rows], dst.at[rows], sems.at[len(copies)]))
    for copy in copies:
        copy.start()
    queue = iter(copies)
    next(queue).wait()
    q = stacked(q_ref[...])
    lefts = []
    size = tokens // cuts[0]
    for i in range(cuts[0]):
        next(queue).wait()
        lefts.append(times(q, g_ref[pl.ds(i * size, size), :], NT))
    left = stacked(jnp.concatenate(lefts, axis=1))
    size = tokens // cuts[1]
    total = None
    for i in range(cuts[1]):
        next(queue).wait()
        at = slice(i * size, (i + 1) * size)
        term = times(left[:, at], a_ref[at, :], NN)
        total = term if total is None else total + term
    size = width // cuts[2]
    for i in range(cuts[2]):
        next(queue).wait()
        at = slice(i * size, (i + 1) * size)
        p_ref[:, at] = total[:, at] + times(q, e_ref[at, :], NT)


def p_local(start_q, activations, out_grads, error_buffer, cuts=(2, 2, 2)):
    return pl.pallas_call(
        functools.partial(p_kernel, cuts=cuts),
        out_shape=(
            jax.ShapeDtypeStruct(start_q.shape, F32),
            pltpu.VMEM(activations.shape, BF16),
            pltpu.VMEM(out_grads.shape, BF16),
            pltpu.VMEM(error_buffer.shape, BF16),
        ),
        in_specs=[HBM, HBM, HBM, HBM],
        out_specs=(VMEM, VMEM, VMEM, VMEM),
        scratch_shapes=[pltpu.VMEM(start_q.shape, F32), pltpu.SemaphoreType.DMA((1 + sum(cuts),))],
        compiler_params=params(),
        name="p_local",
    )(in_hbm(start_q), in_hbm(activations), in_hbm(out_grads), in_hbm(error_buffer))


def merged_rows(i, a_ref, g_ref, e_ref):
    at = slice(i * BLOCK, (i + 1) * BLOCK)
    product = lax.dot_general(a_ref[:, at], g_ref[...], TN, preferred_element_type=F32)
    return product + e_ref[at, :].astype(F32)


def merged_block(i, a, g, e, after):
    def kernel(a_ref, g_ref, e_ref, after_ref, m_ref):
        del after_ref
        m_ref[...] = merged_rows(i, a_ref, g_ref, e_ref)

    return pl.pallas_call(
        kernel,
        out_shape=pltpu.VMEM((BLOCK, e.shape[1]), F32),
        in_specs=[VMEM, VMEM, VMEM, ANY],
        out_specs=VMEM,
        compiler_params=params(),
        cost_estimate=pl.CostEstimate(
            flops=2 * a.shape[0] * BLOCK * g.shape[1], bytes_accessed=0, transcendentals=0
        ),
        name="merged_block",
    )(a, g, e, after)


def orthonormal(rest):
    rows = lax.broadcasted_iota(jnp.int32, (rest.shape[0], 1), 0)
    hat = jnp.zeros_like(rest)
    for j in range(rest.shape[0]):
        row = rest[j : j + 1]
        dots = jnp.sum(row * rest, axis=1, keepdims=True)
        square = dots[j : j + 1]
        hat = jnp.where(rows == j, row / jnp.sqrt(square), hat)
        rest = rest - (dots / square) * row
    return hat


def q_kernel(p_ref, a_ref, g_ref, e_ref, q_ref, hat_ref, m_ref, *, block):
    if block is not None:
        m_ref[...] = merged_rows(block, a_ref, g_ref, e_ref)
    hat = orthonormal(p_ref[...])
    p1, p2, p3 = parts_of(hat)
    zero = jnp.zeros_like(hat)
    hat_ref[...] = jnp.concatenate([p1, p1, p2, p2, p1, p3, zero, zero], axis=0).astype(BF16).T
    stack = stacked(hat)
    left = stacked(times(stack, a_ref[...], NT))
    q_ref[...] = times(stack, e_ref[...], NN) + times(left, g_ref[...], NN)


def q_local(p_sum, a, g, e, block):
    return pl.pallas_call(
        functools.partial(q_kernel, block=block),
        out_shape=(
            jax.ShapeDtypeStruct(p_sum.shape, F32),
            pltpu.VMEM((p_sum.shape[1], 8 * p_sum.shape[0]), BF16),
            pltpu.VMEM((BLOCK, e.shape[1]), F32),
        ),
        in_specs=[VMEM, VMEM, VMEM, VMEM],
        out_specs=(VMEM, VMEM, VMEM),
        compiler_params=params(),
        name="q_local",
    )(p_sum, a, g, e)


def update_kernel(total_ref, hat_ref, *refs, replicas, n):
    m_refs = refs[:n]
    out_hbm, f_hbm, f_ref, out_ref, sems = refs[n:]
    factor = total_ref[...] * (1.0 / replicas)
    f_ref[...] = factor
    copies = [pltpu.make_async_copy(f_ref, f_hbm, sems.at[n])]
    copies[0].start()
    f1, f2, f3 = parts_of(factor)
    zero = jnp.zeros_like(f1)
    lhs = hat_ref[...]
    rhs = jnp.concatenate([f1, f2, f1, f2, f3, f1, zero, zero], axis=0).astype(BF16)
    for i in range(n):
        at = slice(i * BLOCK, (i + 1) * BLOCK)
        update = lax.dot_general(lhs[at, :], rhs, NN, preferred_element_type=F32)
        out_ref[at, :] = (m_refs[i][...] - update).astype(BF16)
        copies.append(pltpu.make_async_copy(out_ref.at[at], out_hbm.at[at], sems.at[i]))
        copies[-1].start()
    for copy in copies:
        copy.wait()


def update(q_total, hat, blocks, replicas):
    n = len(blocks)
    shape = (n * BLOCK, q_total.shape[1])
    return pl.pallas_call(
        functools.partial(update_kernel, replicas=replicas, n=n),
        out_shape=(
            jax.ShapeDtypeStruct(shape, BF16),
            jax.ShapeDtypeStruct(q_total.shape, F32),
        ),
        in_specs=[VMEM] * (2 + n),
        out_specs=(HBM, HBM),
        scratch_shapes=[
            pltpu.VMEM(q_total.shape, F32),
            pltpu.VMEM(shape, BF16),
            pltpu.SemaphoreType.DMA((n + 1,)),
        ],
        compiler_params=params(),
        name="update",
    )(q_total, hat, *blocks)


CORES = 2


def permute(x, target):
    n_row, n_col = lax.axis_size("row"), lax.axis_size("col")
    pairs = []
    for i in range(n_row * n_col):
        row, col = target(*divmod(i, n_col))
        pairs.append((i, (row % n_row) * n_col + col))
    return lax.ppermute(x, AXES, pairs)


def gather_sum(x, groups):
    n = len(groups[0])
    every = jnp.broadcast_to(x[None], (n,) + x.shape)
    every = lax.all_to_all(every, AXES, 0, 0, axis_index_groups=groups, tiled=True)
    terms = [every[i] for i in range(n)]
    while len(terms) > 1:
        terms = [low + high for low, high in zip(terms[0::2], terms[1::2])]
    return terms[0]


def core_scatter(x, core, beside):
    half = x.shape[0] // CORES
    low, high = x[:half], x[half:]
    sent = jnp.where(core == 0, high, low)
    other, extra = lax.optimization_barrier((permute(sent, lambda r, c: (r, c ^ 1)), beside(sent)))
    return jnp.where(core == 0, low, high) + other, extra


def core_gather(x, core, beside):
    other, extra = lax.optimization_barrier((permute(x, lambda r, c: (r, c ^ 1)), beside(x)))
    rows = [jnp.where(core == 0, x, other), jnp.where(core == 0, other, x)]
    return jnp.concatenate(rows, axis=0), extra


def listed(i, step, n):
    side = math.isqrt(n)
    return i % side * side + i // side if step == 0 else i * step % n


def xy_groups(steps):
    n_row, n_col = lax.axis_size("row"), lax.axis_size("col")
    n = n_col // CORES
    return [
        [r * n_col + listed(i, steps[k], n) * CORES + k for i in range(n)]
        for r in range(n_row)
        for k in range(CORES)
    ]


def z_groups(order):
    n_col = lax.axis_size("col")
    return [[r * n_col + c for r in order] for c in range(n_col)]


def on_device(activations, out_grads, error_buffer, start_q):
    replicas = lax.axis_size("row") * lax.axis_size("col")
    core = lax.axis_index("col") & (CORES - 1)
    p, a, g, e = p_local(start_q, activations, out_grads, error_buffer)
    block = lambda i: lambda after: merged_block(i, a, g, e, after)
    p, m0 = core_scatter(p, core, block(0))
    p = gather_sum(gather_sum(p, xy_groups((9, 9))), z_groups([1, 5, 6, 4, 2, 7, 0, 3]))
    p_sum, m1 = core_gather(p, core, block(1))
    q, hat, m2 = q_local(p_sum, a, g, e, 2)
    q, m3 = core_scatter(q, core, block(3))
    q = gather_sum(gather_sum(q, xy_groups((0, 1))), z_groups([1, 2, 0, 7, 6, 3, 5, 4]))
    q_total, m4 = core_gather(q, core, block(4))
    return update(q_total, hat, [m0, m1, m2, m3, m4], replicas)


def solution(mesh):
    return jax.shard_map(
        on_device,
        mesh=mesh,
        in_specs=(P(AXES, None), P(AXES, None), P(AXES, None), P()),
        out_specs=(P(AXES, None), P()),
        check_vma=False,
    )
```

```python
import functools
import math

import jax
import jax.numpy as jnp
from jax import lax
from jax.experimental import pallas as pl
from jax.experimental.pallas import tpu as pltpu
from jax.sharding import PartitionSpec as P

F32, BF16 = jnp.float32, jnp.bfloat16
CUTS = (0, 256, 640, 896, 1280)
VMEM = pl.BlockSpec(memory_space=pltpu.VMEM)
ANY = pl.BlockSpec(memory_space=pl.ANY)
HBM = pl.BlockSpec(memory_space=pltpu.HBM)
AXES = ("row", "col")
NT = (((1,), (1,)), ((), ()))
NN = (((1,), (0,)), ((), ()))
TN = (((0,), (0,)), ((), ()))


def params():
    return pltpu.CompilerParams(vmem_limit_bytes=16 * 1024 * 1024)


def in_hbm(x):
    return pltpu.with_memory_space_constraint(x, pltpu.HBM)


def in_vmem(x):
    return pltpu.with_memory_space_constraint(x, pltpu.VMEM)


def parts_of(x):
    high = x.astype(BF16).astype(F32)
    rest = x - high
    mid = rest.astype(BF16).astype(F32)
    low = (rest - mid).astype(BF16).astype(F32)
    return high, mid, low


def stacked(x):
    high, mid, low = parts_of(x)
    return jnp.concatenate([high, mid, low, jnp.zeros_like(x)], axis=0).astype(BF16)


def times(lhs, rhs, dims):
    out = lax.dot_general(lhs, rhs, dims, preferred_element_type=F32)
    return out[0:8] + (out[8:16] + out[16:24])


def p_kernel(q_hbm, a_hbm, g_hbm, e_hbm, p_ref, a_ref, g_ref, e_ref, q_ref, sems, *, cuts):
    tokens, width = a_ref.shape
    copies = [pltpu.make_async_copy(q_hbm, q_ref, sems.at[0])]
    for src, dst, n in ((g_hbm, g_ref, cuts[0]), (a_hbm, a_ref, cuts[1]), (e_hbm, e_ref, cuts[2])):
        size = src.shape[0] // n
        for i in range(n):
            rows = pl.ds(i * size, size)
            copies.append(pltpu.make_async_copy(src.at[rows], dst.at[rows], sems.at[len(copies)]))
    for copy in copies:
        copy.start()
    queue = iter(copies)
    next(queue).wait()
    q = stacked(q_ref[...])
    lefts = []
    size = tokens // cuts[0]
    for i in range(cuts[0]):
        next(queue).wait()
        lefts.append(times(q, g_ref[pl.ds(i * size, size), :], NT))
    left = stacked(jnp.concatenate(lefts, axis=1))
    size = tokens // cuts[1]
    total = None
    for i in range(cuts[1]):
        next(queue).wait()
        at = slice(i * size, (i + 1) * size)
        term = times(left[:, at], a_ref[at, :], NN)
        total = term if total is None else total + term
    size = width // cuts[2]
    for i in range(cuts[2]):
        next(queue).wait()
        at = slice(i * size, (i + 1) * size)
        p_ref[:, at] = total[:, at] + times(q, e_ref[at, :], NT)


def p_local(start_q, activations, out_grads, error_buffer, cuts=(2, 2, 2)):
    return pl.pallas_call(
        functools.partial(p_kernel, cuts=cuts),
        out_shape=(
            jax.ShapeDtypeStruct(start_q.shape, F32),
            pltpu.VMEM(activations.shape, BF16),
            pltpu.VMEM(out_grads.shape, BF16),
            pltpu.VMEM(error_buffer.shape, BF16),
        ),
        in_specs=[HBM, HBM, HBM, HBM],
        out_specs=(VMEM, VMEM, VMEM, VMEM),
        scratch_shapes=[pltpu.VMEM(start_q.shape, F32), pltpu.SemaphoreType.DMA((1 + sum(cuts),))],
        compiler_params=params(),
        name="p_local",
    )(in_hbm(start_q), in_hbm(activations), in_hbm(out_grads), in_hbm(error_buffer))


def merged_rows(rows, a_ref, g_ref, e_ref):
    at = slice(*rows)
    product = lax.dot_general(a_ref[:, at], g_ref[...], TN, preferred_element_type=F32)
    return product + e_ref[at, :].astype(F32)


def merged_block(rows, a, g, e, after):
    def kernel(a_ref, g_ref, e_ref, after_ref, m_ref):
        del after_ref
        m_ref[...] = merged_rows(rows, a_ref, g_ref, e_ref)

    return pl.pallas_call(
        kernel,
        out_shape=pltpu.VMEM((rows[1] - rows[0], e.shape[1]), F32),
        in_specs=[VMEM, VMEM, VMEM, ANY],
        out_specs=VMEM,
        compiler_params=params(),
        cost_estimate=pl.CostEstimate(
            flops=2 * a.shape[0] * (rows[1] - rows[0]) * g.shape[1], bytes_accessed=0, transcendentals=0
        ),
        name="merged_block",
    )(a, g, e, after)


def block_on_core(which, rows, a, g, e, after, before=None):
    carried = [] if before is None else [in_vmem(before)]

    def kernel(a_ref, g_ref, e_ref, after_ref, *refs):
        del after_ref

        @pl.when(lax.axis_index("col") % CORES == which)
        def _():
            refs[-1][...] = merged_rows(rows, a_ref, g_ref, e_ref)

    return pl.pallas_call(
        kernel,
        out_shape=pltpu.VMEM((rows[1] - rows[0], e.shape[1]), F32),
        in_specs=[VMEM, VMEM, VMEM, ANY] + [VMEM] * len(carried),
        out_specs=VMEM,
        input_output_aliases={4: 0} if carried else {},
        compiler_params=params(),
        cost_estimate=pl.CostEstimate(
            flops=2 * a.shape[0] * (rows[1] - rows[0]) * g.shape[1], bytes_accessed=0, transcendentals=0
        ),
        name="block_on_core",
    )(a, g, e, after, *carried)


def orthonormal(vectors):
    n, width = vectors.shape
    rows = lax.broadcasted_iota(jnp.int32, (n, 128), 0)
    lanes = lax.broadcasted_iota(jnp.int32, (n, 128), 1)
    rest = jnp.concatenate([vectors, (rows == lanes).astype(F32)], axis=1)
    rows = lax.broadcasted_iota(jnp.int32, (n, 1), 0)
    hat = jnp.zeros_like(rest)
    for j in range(n):
        row = rest[j : j + 1]
        dots = jnp.sum(row[:, :width] * rest[:, :width], axis=1, keepdims=True)
        square = dots[j : j + 1]
        hat = jnp.where(rows == j, row / jnp.sqrt(square), hat)
        rest = rest - (dots / square) * row
    return hat[:, :width], hat[:, width:]


def q_kernel(p_ref, a_ref, g_ref, e_ref, q_ref, hat_ref):
    p_sum = p_ref[...]
    stack = stacked(p_sum)
    left = stacked(times(stack, a_ref[...], NT))
    product = times(stack, e_ref[...], NN) + times(left, g_ref[...], NN)
    hat, factors = orthonormal(p_sum)
    p1, p2, p3 = parts_of(hat)
    zero = jnp.zeros_like(hat)
    hat_ref[...] = jnp.concatenate([p1, p1, p2, p2, p1, p3, zero, zero], axis=0).astype(BF16)
    total = factors[:, 0:1] * product[0:1]
    for j in range(1, p_sum.shape[0]):
        total = total + factors[:, j : j + 1] * product[j : j + 1]
    q_ref[...] = total


def q_local(p_sum, a, g, e):
    return pl.pallas_call(
        q_kernel,
        out_shape=(
            jax.ShapeDtypeStruct(p_sum.shape, F32),
            pltpu.VMEM((8 * p_sum.shape[0], p_sum.shape[1]), BF16),
        ),
        in_specs=[VMEM, VMEM, VMEM, VMEM],
        out_specs=(VMEM, VMEM),
        compiler_params=params(),
        name="q_local",
    )(p_sum, a, g, e)


def update_kernel(total_ref, hat_ref, *refs, replicas, n):
    m_refs = refs[:n]
    out_hbm, f_hbm, f_ref, out_ref, sems = refs[n:]
    factor = total_ref[...] * (1.0 / replicas)
    f_ref[...] = factor
    copies = [pltpu.make_async_copy(f_ref, f_hbm, sems.at[n])]
    copies[0].start()
    f1, f2, f3 = parts_of(factor)
    zero = jnp.zeros_like(f1)
    lhs = hat_ref[...]
    rhs = jnp.concatenate([f1, f2, f1, f2, f3, f1, zero, zero], axis=0).astype(BF16)
    start = 0
    for i, m_ref in enumerate(m_refs):
        at = slice(start, start + m_ref.shape[0])
        start = at.stop
        change = lax.dot_general(lhs[:, at], rhs, TN, preferred_element_type=F32)
        out_ref[at, :] = (m_ref[...] - change).astype(BF16)
        copies.append(pltpu.make_async_copy(out_ref.at[at], out_hbm.at[at], sems.at[i]))
        copies[-1].start()
    for copy in copies:
        copy.wait()


def update(q_total, hat, blocks, replicas):
    n = len(blocks)
    shape = (sum(block.shape[0] for block in blocks), q_total.shape[1])
    return pl.pallas_call(
        functools.partial(update_kernel, replicas=replicas, n=n),
        out_shape=(
            jax.ShapeDtypeStruct(shape, BF16),
            jax.ShapeDtypeStruct(q_total.shape, F32),
        ),
        in_specs=[VMEM] * (2 + n),
        out_specs=(HBM, HBM),
        scratch_shapes=[
            pltpu.VMEM(q_total.shape, F32),
            pltpu.VMEM(shape, BF16),
            pltpu.SemaphoreType.DMA((n + 1,)),
        ],
        compiler_params=params(),
        name="update",
    )(q_total, hat, *blocks)


CORES = 2


def permute(x, target):
    n_row, n_col = lax.axis_size("row"), lax.axis_size("col")
    pairs = []
    for i in range(n_row * n_col):
        row, col = target(*divmod(i, n_col))
        pairs.append((i, (row % n_row) * n_col + col))
    return lax.ppermute(x, AXES, pairs)


def gather_sum(x, groups):
    n = len(groups[0])
    every = jnp.broadcast_to(x[None], (n,) + x.shape)
    every = lax.all_to_all(every, AXES, 0, 0, axis_index_groups=groups, tiled=True)
    terms = [every[i] for i in range(n)]
    while len(terms) > 1:
        terms = [low + high for low, high in zip(terms[0::2], terms[1::2])]
    return terms[0]


def core_scatter(x, core, beside):
    half = x.shape[0] // CORES
    low, high = x[:half], x[half:]
    sent = jnp.where(core == 0, high, low)
    other, extra = lax.optimization_barrier((permute(sent, lambda r, c: (r, c ^ 1)), beside(sent)))
    return jnp.where(core == 0, low, high) + other, extra


def core_gather(x, core, beside):
    other, extra = lax.optimization_barrier((permute(x, lambda r, c: (r, c ^ 1)), beside(x)))
    rows = [jnp.where(core == 0, x, other), jnp.where(core == 0, other, x)]
    return jnp.concatenate(rows, axis=0), extra


def listed(i, step, n):
    side = math.isqrt(n)
    return i % side * side + i // side if step == 0 else i * step % n


def xy_groups(steps):
    n_row, n_col = lax.axis_size("row"), lax.axis_size("col")
    n = n_col // CORES
    return [
        [r * n_col + listed(i, steps[k], n) * CORES + k for i in range(n)]
        for r in range(n_row)
        for k in range(CORES)
    ]


def z_groups(order):
    n_col = lax.axis_size("col")
    return [[r * n_col + c for r in order] for c in range(n_col)]


def on_device(activations, out_grads, error_buffer, start_q):
    replicas = lax.axis_size("row") * lax.axis_size("col")
    core = lax.axis_index("col") & (CORES - 1)
    p, a, g, e = p_local(start_q, activations, out_grads, error_buffer)
    rows = list(zip(CUTS[:-1], CUTS[1:]))

    def gather(x, rows):
        x, block = lax.optimization_barrier((x, block_on_core(1, rows, a, g, e, x)))
        return core_gather(
            x, core, lambda after: block_on_core(0, rows, a, g, e, after, block)
        )

    p, m0 = core_scatter(p, core, lambda after: merged_block(rows[0], a, g, e, after))
    p = gather_sum(gather_sum(p, xy_groups((9, 9))), z_groups([1, 5, 6, 4, 2, 7, 0, 3]))
    p_sum, m1 = gather(p, rows[1])
    q, hat = q_local(p_sum, a, g, e)
    q, m2 = core_scatter(q, core, lambda after: merged_block(rows[2], a, g, e, after))
    q = gather_sum(gather_sum(q, xy_groups((0, 1))), z_groups([1, 2, 0, 7, 6, 3, 5, 4]))
    q_total, m3 = gather(q, rows[3])
    return update(q_total, hat, [m0, m1, m2, m3], replicas)


def solution(mesh):
    return jax.shard_map(
        on_device,
        mesh=mesh,
        in_specs=(P(AXES, None), P(AXES, None), P(AXES, None), P()),
        out_specs=(P(AXES, None), P()),
        check_vma=False,
    )
```

```python
import functools
import math

import jax
import jax.numpy as jnp
from jax import lax
from jax.experimental import pallas as pl
from jax.experimental.pallas import tpu as pltpu
from jax.sharding import PartitionSpec as P

F32, BF16 = jnp.float32, jnp.bfloat16
CUTS = (0, 256, 640, 896, 1280)
PIECE = 128
VMEM = pl.BlockSpec(memory_space=pltpu.VMEM)
ANY = pl.BlockSpec(memory_space=pl.ANY)
HBM = pl.BlockSpec(memory_space=pltpu.HBM)
AXES = ("row", "col")
NT = (((1,), (1,)), ((), ()))
NN = (((1,), (0,)), ((), ()))
TN = (((0,), (0,)), ((), ()))


def params():
    return pltpu.CompilerParams(vmem_limit_bytes=16 * 1024 * 1024)


def in_hbm(x):
    return pltpu.with_memory_space_constraint(x, pltpu.HBM)


def in_vmem(x):
    return pltpu.with_memory_space_constraint(x, pltpu.VMEM)


def parts_of(x):
    high = x.astype(BF16).astype(F32)
    rest = x - high
    mid = rest.astype(BF16).astype(F32)
    low = (rest - mid).astype(BF16).astype(F32)
    return high, mid, low


def stacked(x):
    high, mid, low = parts_of(x)
    return jnp.concatenate([high, mid, low, jnp.zeros_like(x)], axis=0).astype(BF16)


def times(lhs, rhs, dims):
    out = lax.dot_general(lhs, rhs, dims, preferred_element_type=F32)
    return out[0:8] + (out[8:16] + out[16:24])


def p_kernel(q_hbm, a_hbm, g_hbm, e_hbm, p_ref, a_ref, g_ref, e_ref, q_ref, sems, *, cuts):
    tokens, width = a_ref.shape
    copies = [pltpu.make_async_copy(q_hbm, q_ref, sems.at[0])]
    for src, dst, n in ((g_hbm, g_ref, cuts[0]), (a_hbm, a_ref, cuts[1]), (e_hbm, e_ref, cuts[2])):
        size = src.shape[0] // n
        for i in range(n):
            rows = pl.ds(i * size, size)
            copies.append(pltpu.make_async_copy(src.at[rows], dst.at[rows], sems.at[len(copies)]))
    for copy in copies:
        copy.start()
    queue = iter(copies)
    next(queue).wait()
    q = stacked(q_ref[...])
    lefts = []
    size = tokens // cuts[0]
    for i in range(cuts[0]):
        next(queue).wait()
        lefts.append(times(q, g_ref[pl.ds(i * size, size), :], NT))
    left = stacked(jnp.concatenate(lefts, axis=1))
    size = tokens // cuts[1]
    total = None
    for i in range(cuts[1]):
        next(queue).wait()
        at = slice(i * size, (i + 1) * size)
        term = times(left[:, at], a_ref[at, :], NN)
        total = term if total is None else total + term
    size = width // cuts[2]
    for i in range(cuts[2]):
        next(queue).wait()
        at = slice(i * size, (i + 1) * size)
        p_ref[:, at] = total[:, at] + times(q, e_ref[at, :], NT)


def p_local(start_q, activations, out_grads, error_buffer, cuts=(2, 2, 2)):
    return pl.pallas_call(
        functools.partial(p_kernel, cuts=cuts),
        out_shape=(
            jax.ShapeDtypeStruct(start_q.shape, F32),
            pltpu.VMEM(activations.shape, BF16),
            pltpu.VMEM(out_grads.shape, BF16),
            pltpu.VMEM(error_buffer.shape, BF16),
        ),
        in_specs=[HBM, HBM, HBM, HBM],
        out_specs=(VMEM, VMEM, VMEM, VMEM),
        scratch_shapes=[pltpu.VMEM(start_q.shape, F32), pltpu.SemaphoreType.DMA((1 + sum(cuts),))],
        compiler_params=params(),
        name="p_local",
    )(in_hbm(start_q), in_hbm(activations), in_hbm(out_grads), in_hbm(error_buffer))


def merged_rows(rows, a_ref, g_ref, e_ref):
    at = slice(*rows)
    product = lax.dot_general(a_ref[:, at], g_ref[...], TN, preferred_element_type=F32)
    return product + e_ref[at, :].astype(F32)


def merged_block(rows, a, g, e, after):
    def kernel(a_ref, g_ref, e_ref, after_ref, m_ref):
        del after_ref
        m_ref[...] = merged_rows(rows, a_ref, g_ref, e_ref)

    return pl.pallas_call(
        kernel,
        out_shape=pltpu.VMEM((rows[1] - rows[0], e.shape[1]), F32),
        in_specs=[VMEM, VMEM, VMEM, ANY],
        out_specs=VMEM,
        compiler_params=params(),
        cost_estimate=pl.CostEstimate(
            flops=2 * a.shape[0] * (rows[1] - rows[0]) * g.shape[1], bytes_accessed=0, transcendentals=0
        ),
        name="merged_block",
    )(a, g, e, after)


def block_on_core(which, rows, a, g, e, after, before=None):
    carried = [] if before is None else [in_vmem(before)]

    def kernel(a_ref, g_ref, e_ref, after_ref, *refs):
        del after_ref

        @pl.when(lax.axis_index("col") % CORES == which)
        def _():
            refs[-1][...] = merged_rows(rows, a_ref, g_ref, e_ref)

    return pl.pallas_call(
        kernel,
        out_shape=pltpu.VMEM((rows[1] - rows[0], e.shape[1]), F32),
        in_specs=[VMEM, VMEM, VMEM, ANY] + [VMEM] * len(carried),
        out_specs=VMEM,
        input_output_aliases={4: 0} if carried else {},
        compiler_params=params(),
        cost_estimate=pl.CostEstimate(
            flops=2 * a.shape[0] * (rows[1] - rows[0]) * g.shape[1], bytes_accessed=0, transcendentals=0
        ),
        name="block_on_core",
    )(a, g, e, after, *carried)


def orthonormal(vectors):
    n, width = vectors.shape
    rows = lax.broadcasted_iota(jnp.int32, (n, 128), 0)
    lanes = lax.broadcasted_iota(jnp.int32, (n, 128), 1)
    rest = jnp.concatenate([vectors, (rows == lanes).astype(F32)], axis=1)
    rows = lax.broadcasted_iota(jnp.int32, (n, 1), 0)
    hat = jnp.zeros_like(rest)
    for j in range(n):
        row = rest[j : j + 1]
        dots = jnp.sum(row[:, :width] * rest[:, :width], axis=1, keepdims=True)
        square = dots[j : j + 1]
        hat = jnp.where(rows == j, row / jnp.sqrt(square), hat)
        rest = rest - (dots / square) * row
    return hat[:, :width], hat[:, width:]


def q_kernel(p_ref, a_ref, g_ref, e_ref, q_ref, hat_ref):
    p_sum = p_ref[...]
    stack = stacked(p_sum)
    left = stacked(times(stack, a_ref[...], NT))
    product = times(stack, e_ref[...], NN) + times(left, g_ref[...], NN)
    hat, factors = orthonormal(p_sum)
    p1, p2, p3 = parts_of(hat)
    zero = jnp.zeros_like(hat)
    hat_ref[...] = jnp.concatenate([p1, p1, p2, p2, p1, p3, zero, zero], axis=0).astype(BF16).T
    total = factors[:, 0:1] * product[0:1]
    for j in range(1, p_sum.shape[0]):
        total = total + factors[:, j : j + 1] * product[j : j + 1]
    q_ref[...] = total


def q_local(p_sum, a, g, e):
    return pl.pallas_call(
        q_kernel,
        out_shape=(
            jax.ShapeDtypeStruct(p_sum.shape, F32),
            pltpu.VMEM((p_sum.shape[1], 8 * p_sum.shape[0]), BF16),
        ),
        in_specs=[VMEM, VMEM, VMEM, VMEM],
        out_specs=(VMEM, VMEM),
        compiler_params=params(),
        name="q_local",
    )(p_sum, a, g, e)


def update_kernel(total_ref, hat_ref, *refs, replicas, n):
    m_refs = refs[:n]
    out_hbm, f_hbm, f_ref, out_ref, sems = refs[n:]
    factor = total_ref[...] * (1.0 / replicas)
    f_ref[...] = factor
    copies = [pltpu.make_async_copy(f_ref, f_hbm, sems.at[0])]
    copies[0].start()
    f1, f2, f3 = parts_of(factor)
    zero = jnp.zeros_like(f1)
    lhs = hat_ref[...]
    rhs = jnp.concatenate([f1, f2, f1, f2, f3, f1, zero, zero], axis=0).astype(BF16)
    start = 0
    for m_ref in m_refs:
        for offset in range(0, m_ref.shape[0], PIECE):
            at = slice(start, start + PIECE)
            start = at.stop
            change = lax.dot_general(lhs[at, :], rhs, NN, preferred_element_type=F32)
            out_ref[at, :] = (m_ref[offset : offset + PIECE, :] - change).astype(BF16)
            sem = sems.at[len(copies)]
            copies.append(pltpu.make_async_copy(out_ref.at[at], out_hbm.at[at], sem))
            copies[-1].start()
    for copy in copies:
        copy.wait()


def update(q_total, hat, blocks, replicas):
    n = len(blocks)
    shape = (sum(block.shape[0] for block in blocks), q_total.shape[1])
    return pl.pallas_call(
        functools.partial(update_kernel, replicas=replicas, n=n),
        out_shape=(
            jax.ShapeDtypeStruct(shape, BF16),
            jax.ShapeDtypeStruct(q_total.shape, F32),
        ),
        in_specs=[VMEM] * (2 + n),
        out_specs=(HBM, HBM),
        scratch_shapes=[
            pltpu.VMEM(q_total.shape, F32),
            pltpu.VMEM(shape, BF16),
            pltpu.SemaphoreType.DMA((shape[0] // PIECE + 1,)),
        ],
        compiler_params=params(),
        name="update",
    )(q_total, hat, *blocks)


CORES = 2


def permute(x, target):
    n_row, n_col = lax.axis_size("row"), lax.axis_size("col")
    pairs = []
    for i in range(n_row * n_col):
        row, col = target(*divmod(i, n_col))
        pairs.append((i, (row % n_row) * n_col + col))
    return lax.ppermute(x, AXES, pairs)


def gather_sum(x, groups):
    n = len(groups[0])
    every = jnp.broadcast_to(x[None], (n,) + x.shape)
    every = lax.all_to_all(every, AXES, 0, 0, axis_index_groups=groups, tiled=True)
    terms = [every[i] for i in range(n)]
    while len(terms) > 1:
        terms = [low + high for low, high in zip(terms[0::2], terms[1::2])]
    return terms[0]


def core_scatter(x, core, beside):
    half = x.shape[0] // CORES
    low, high = x[:half], x[half:]
    sent = jnp.where(core == 0, high, low)
    other, extra = lax.optimization_barrier((permute(sent, lambda r, c: (r, c ^ 1)), beside(sent)))
    return jnp.where(core == 0, low, high) + other, extra


def core_gather(x, core, beside):
    other, extra = lax.optimization_barrier((permute(x, lambda r, c: (r, c ^ 1)), beside(x)))
    rows = [jnp.where(core == 0, x, other), jnp.where(core == 0, other, x)]
    return jnp.concatenate(rows, axis=0), extra


def listed(i, step, n):
    side = math.isqrt(n)
    return i % side * side + i // side if step == 0 else i * step % n


def xy_groups(steps):
    n_row, n_col = lax.axis_size("row"), lax.axis_size("col")
    n = n_col // CORES
    return [
        [r * n_col + listed(i, steps[k], n) * CORES + k for i in range(n)]
        for r in range(n_row)
        for k in range(CORES)
    ]


def z_groups(order):
    n_col = lax.axis_size("col")
    return [[r * n_col + c for r in order] for c in range(n_col)]


def on_device(activations, out_grads, error_buffer, start_q):
    replicas = lax.axis_size("row") * lax.axis_size("col")
    core = lax.axis_index("col") & (CORES - 1)
    p, a, g, e = p_local(start_q, activations, out_grads, error_buffer)
    rows = list(zip(CUTS[:-1], CUTS[1:]))

    def gather(x, rows):
        x, block = lax.optimization_barrier((x, block_on_core(1, rows, a, g, e, x)))
        return core_gather(
            x, core, lambda after: block_on_core(0, rows, a, g, e, after, block)
        )

    p, m0 = core_scatter(p, core, lambda after: merged_block(rows[0], a, g, e, after))
    p = gather_sum(gather_sum(p, xy_groups((9, 9))), z_groups([1, 5, 6, 4, 2, 7, 0, 3]))
    p_sum, m1 = gather(p, rows[1])
    q, hat = q_local(p_sum, a, g, e)
    q, m2 = core_scatter(q, core, lambda after: merged_block(rows[2], a, g, e, after))
    q = gather_sum(gather_sum(q, xy_groups((0, 1))), z_groups([1, 2, 0, 7, 6, 3, 5, 4]))
    q_total, m3 = gather(q, rows[3])
    return update(q_total, hat, [m0, m1, m2, m3], replicas)


def solution(mesh):
    return jax.shard_map(
        on_device,
        mesh=mesh,
        in_specs=(P(AXES, None), P(AXES, None), P(AXES, None), P()),
        out_specs=(P(AXES, None), P()),
        check_vma=False,
    )
```

```python
import functools
import math

import jax
import jax.numpy as jnp
from jax import lax
from jax.experimental import pallas as pl
from jax.experimental.pallas import tpu as pltpu
from jax.sharding import PartitionSpec as P

F32, BF16 = jnp.float32, jnp.bfloat16
CUTS = (0, 256, 640, 896, 1280)
PIECE = 128
VMEM = pl.BlockSpec(memory_space=pltpu.VMEM)
ANY = pl.BlockSpec(memory_space=pl.ANY)
HBM = pl.BlockSpec(memory_space=pltpu.HBM)
AXES = ("row", "col")
NT = (((1,), (1,)), ((), ()))
NN = (((1,), (0,)), ((), ()))
TN = (((0,), (0,)), ((), ()))


def params():
    return pltpu.CompilerParams(vmem_limit_bytes=16 * 1024 * 1024)


def in_hbm(x):
    return pltpu.with_memory_space_constraint(x, pltpu.HBM)


def in_vmem(x):
    return pltpu.with_memory_space_constraint(x, pltpu.VMEM)


def parts_of(x):
    high = x.astype(BF16).astype(F32)
    rest = x - high
    mid = rest.astype(BF16).astype(F32)
    low = (rest - mid).astype(BF16).astype(F32)
    return high, mid, low


def stacked(x):
    high, mid, low = parts_of(x)
    return jnp.concatenate([high, mid, low, jnp.zeros_like(x)], axis=0).astype(BF16)


def times(lhs, rhs, dims):
    out = lax.dot_general(lhs, rhs, dims, preferred_element_type=F32)
    return out[0:8] + (out[8:16] + out[16:24])


def ranges(size, n):
    blocks = size // 256
    starts = [256 * -(-blocks * i // n) for i in range(n + 1)]
    return [pl.ds(low, high - low) for low, high in zip(starts[:-1], starts[1:])]


def p_kernel(q_hbm, a_hbm, g_hbm, e_hbm, p_ref, a_ref, g_ref, e_ref, q_ref, sems, *, cuts):
    tokens, width = a_ref.shape
    copies = [pltpu.make_async_copy(q_hbm, q_ref, sems.at[0])]
    for src, dst, n in ((g_hbm, g_ref, cuts[0]), (a_hbm, a_ref, cuts[1]), (e_hbm, e_ref, cuts[2])):
        for rows in ranges(src.shape[0], n):
            copies.append(pltpu.make_async_copy(src.at[rows], dst.at[rows], sems.at[len(copies)]))
    for copy in copies:
        copy.start()
    queue = iter(copies)
    next(queue).wait()
    q = stacked(q_ref[...])
    lefts = []
    size = tokens // cuts[0]
    for i in range(cuts[0]):
        next(queue).wait()
        lefts.append(times(q, g_ref[pl.ds(i * size, size), :], NT))
    left = stacked(jnp.concatenate(lefts, axis=1))
    size = tokens // cuts[1]
    total = None
    for i in range(cuts[1]):
        next(queue).wait()
        at = slice(i * size, (i + 1) * size)
        term = times(left[:, at], a_ref[at, :], NN)
        total = term if total is None else total + term
    for rows in ranges(width, cuts[2]):
        next(queue).wait()
        at = slice(rows.start, rows.start + rows.size)
        p_ref[:, at] = total[:, at] + times(q, e_ref[at, :], NT)


def p_local(start_q, activations, out_grads, error_buffer, cuts=(2, 2, 2)):
    return pl.pallas_call(
        functools.partial(p_kernel, cuts=cuts),
        out_shape=(
            jax.ShapeDtypeStruct(start_q.shape, F32),
            pltpu.VMEM(activations.shape, BF16),
            pltpu.VMEM(out_grads.shape, BF16),
            pltpu.VMEM(error_buffer.shape, BF16),
        ),
        in_specs=[HBM, HBM, HBM, HBM],
        out_specs=(VMEM, VMEM, VMEM, VMEM),
        scratch_shapes=[pltpu.VMEM(start_q.shape, F32), pltpu.SemaphoreType.DMA((1 + sum(cuts),))],
        compiler_params=params(),
        name="p_local",
    )(in_hbm(start_q), in_hbm(activations), in_hbm(out_grads), in_hbm(error_buffer))


def merged_rows(rows, a_ref, g_ref, e_ref):
    at = slice(*rows)
    product = lax.dot_general(a_ref[:, at], g_ref[...], TN, preferred_element_type=F32)
    return product + e_ref[at, :].astype(F32)


def merged_block(rows, a, g, e, after):
    def kernel(a_ref, g_ref, e_ref, after_ref, m_ref):
        del after_ref
        m_ref[...] = merged_rows(rows, a_ref, g_ref, e_ref)

    return pl.pallas_call(
        kernel,
        out_shape=pltpu.VMEM((rows[1] - rows[0], e.shape[1]), F32),
        in_specs=[VMEM, VMEM, VMEM, ANY],
        out_specs=VMEM,
        compiler_params=params(),
        cost_estimate=pl.CostEstimate(
            flops=2 * a.shape[0] * (rows[1] - rows[0]) * g.shape[1], bytes_accessed=0, transcendentals=0
        ),
        name="merged_block",
    )(a, g, e, after)


def block_on_core(which, rows, a, g, e, after, before=None):
    carried = [] if before is None else [in_vmem(before)]

    def kernel(a_ref, g_ref, e_ref, after_ref, *refs):
        del after_ref

        @pl.when(lax.axis_index("col") % CORES == which)
        def _():
            refs[-1][...] = merged_rows(rows, a_ref, g_ref, e_ref)

    return pl.pallas_call(
        kernel,
        out_shape=pltpu.VMEM((rows[1] - rows[0], e.shape[1]), F32),
        in_specs=[VMEM, VMEM, VMEM, ANY] + [VMEM] * len(carried),
        out_specs=VMEM,
        input_output_aliases={4: 0} if carried else {},
        compiler_params=params(),
        cost_estimate=pl.CostEstimate(
            flops=2 * a.shape[0] * (rows[1] - rows[0]) * g.shape[1], bytes_accessed=0, transcendentals=0
        ),
        name="block_on_core",
    )(a, g, e, after, *carried)


def orthonormal(vectors):
    n, width = vectors.shape
    rows = lax.broadcasted_iota(jnp.int32, (n, 128), 0)
    lanes = lax.broadcasted_iota(jnp.int32, (n, 128), 1)
    rest = jnp.concatenate([vectors, (rows == lanes).astype(F32)], axis=1)
    rows = lax.broadcasted_iota(jnp.int32, (n, 1), 0)
    hat = jnp.zeros_like(rest)
    for j in range(n):
        row = rest[j : j + 1]
        dots = jnp.sum(row[:, :width] * rest[:, :width], axis=1, keepdims=True)
        square = dots[j : j + 1]
        hat = jnp.where(rows == j, row / jnp.sqrt(square), hat)
        rest = rest - (dots / square) * row
    return hat[:, :width], hat[:, width:]


def q_kernel(p_ref, a_ref, g_ref, e_ref, q_ref, hat_ref):
    p_sum = p_ref[...]
    stack = stacked(p_sum)
    left = stacked(times(stack, a_ref[...], NT))
    product = times(stack, e_ref[...], NN) + times(left, g_ref[...], NN)
    hat, factors = orthonormal(p_sum)
    p1, p2, p3 = parts_of(hat)
    zero = jnp.zeros_like(hat)
    hat_ref[...] = jnp.concatenate([p1, p1, p2, p2, p1, p3, zero, zero], axis=0).astype(BF16).T
    total = factors[:, 0:1] * product[0:1]
    for j in range(1, p_sum.shape[0]):
        total = total + factors[:, j : j + 1] * product[j : j + 1]
    q_ref[...] = total


def q_local(p_sum, a, g, e):
    return pl.pallas_call(
        q_kernel,
        out_shape=(
            jax.ShapeDtypeStruct(p_sum.shape, F32),
            pltpu.VMEM((p_sum.shape[1], 8 * p_sum.shape[0]), BF16),
        ),
        in_specs=[VMEM, VMEM, VMEM, VMEM],
        out_specs=(VMEM, VMEM),
        compiler_params=params(),
        name="q_local",
    )(p_sum, a, g, e)


def update_kernel(total_ref, hat_ref, *refs, replicas, n):
    m_refs = refs[:n]
    out_hbm, f_hbm, f_ref, out_ref, sems = refs[n:]
    factor = total_ref[...] * (1.0 / replicas)
    f_ref[...] = factor
    copies = [pltpu.make_async_copy(f_ref, f_hbm, sems.at[0])]
    copies[0].start()
    f1, f2, f3 = parts_of(factor)
    zero = jnp.zeros_like(f1)
    lhs = hat_ref[...]
    rhs = jnp.concatenate([f1, f2, f1, f2, f3, f1, zero, zero], axis=0).astype(BF16)
    start = 0
    for m_ref in m_refs:
        for offset in range(0, m_ref.shape[0], PIECE):
            at = slice(start, start + PIECE)
            start = at.stop
            change = lax.dot_general(lhs[at, :], rhs, NN, preferred_element_type=F32)
            out_ref[at, :] = (m_ref[offset : offset + PIECE, :] - change).astype(BF16)
            sem = sems.at[len(copies)]
            copies.append(pltpu.make_async_copy(out_ref.at[at], out_hbm.at[at], sem))
            copies[-1].start()
    for copy in copies:
        copy.wait()


def update(q_total, hat, blocks, replicas):
    n = len(blocks)
    shape = (sum(block.shape[0] for block in blocks), q_total.shape[1])
    return pl.pallas_call(
        functools.partial(update_kernel, replicas=replicas, n=n),
        out_shape=(
            jax.ShapeDtypeStruct(shape, BF16),
            jax.ShapeDtypeStruct(q_total.shape, F32),
        ),
        in_specs=[VMEM] * (2 + n),
        out_specs=(HBM, HBM),
        scratch_shapes=[
            pltpu.VMEM(q_total.shape, F32),
            pltpu.VMEM(shape, BF16),
            pltpu.SemaphoreType.DMA((shape[0] // PIECE + 1,)),
        ],
        compiler_params=params(),
        name="update",
    )(q_total, hat, *blocks)


CORES = 2


def permute(x, target):
    n_row, n_col = lax.axis_size("row"), lax.axis_size("col")
    pairs = []
    for i in range(n_row * n_col):
        row, col = target(*divmod(i, n_col))
        pairs.append((i, (row % n_row) * n_col + col))
    return lax.ppermute(x, AXES, pairs)


def gather_sum(x, groups):
    n = len(groups[0])
    every = jnp.broadcast_to(x[None], (n,) + x.shape)
    every = lax.all_to_all(every, AXES, 0, 0, axis_index_groups=groups, tiled=True)
    terms = [every[i] for i in range(n)]
    while len(terms) > 1:
        terms = [low + high for low, high in zip(terms[0::2], terms[1::2])]
    return terms[0]


def core_scatter(x, core, beside):
    half = x.shape[0] // CORES
    low, high = x[:half], x[half:]
    sent = jnp.where(core == 0, high, low)
    other, extra = lax.optimization_barrier((permute(sent, lambda r, c: (r, c ^ 1)), beside(sent)))
    return jnp.where(core == 0, low, high) + other, extra


def core_gather(x, core, beside):
    other, extra = lax.optimization_barrier((permute(x, lambda r, c: (r, c ^ 1)), beside(x)))
    rows = [jnp.where(core == 0, x, other), jnp.where(core == 0, other, x)]
    return jnp.concatenate(rows, axis=0), extra


def listed(i, step, n):
    side = math.isqrt(n)
    return i % side * side + i // side if step == 0 else i * step % n


def xy_groups(steps):
    n_row, n_col = lax.axis_size("row"), lax.axis_size("col")
    n = n_col // CORES
    return [
        [r * n_col + listed(i, steps[k], n) * CORES + k for i in range(n)]
        for r in range(n_row)
        for k in range(CORES)
    ]


def z_groups(order):
    n_col = lax.axis_size("col")
    return [[r * n_col + c for r in order] for c in range(n_col)]


def on_device(activations, out_grads, error_buffer, start_q):
    replicas = lax.axis_size("row") * lax.axis_size("col")
    core = lax.axis_index("col") & (CORES - 1)
    p, a, g, e = p_local(start_q, activations, out_grads, error_buffer)
    rows = list(zip(CUTS[:-1], CUTS[1:]))

    def gather(x, rows):
        x, block = lax.optimization_barrier((x, block_on_core(1, rows, a, g, e, x)))
        return core_gather(
            x, core, lambda after: block_on_core(0, rows, a, g, e, after, block)
        )

    p, m0 = core_scatter(p, core, lambda after: merged_block(rows[0], a, g, e, after))
    p = gather_sum(gather_sum(p, xy_groups((9, 9))), z_groups([1, 5, 6, 4, 2, 7, 0, 3]))
    p_sum, m1 = gather(p, rows[1])
    q, hat = q_local(p_sum, a, g, e)
    q, m2 = core_scatter(q, core, lambda after: merged_block(rows[2], a, g, e, after))
    q = gather_sum(gather_sum(q, xy_groups((0, 1))), z_groups([1, 2, 0, 7, 6, 3, 5, 4]))
    q_total, m3 = gather(q, rows[3])
    return update(q_total, hat, [m0, m1, m2, m3], replicas)


def solution(mesh):
    return jax.shard_map(
        on_device,
        mesh=mesh,
        in_specs=(P(AXES, None), P(AXES, None), P(AXES, None), P()),
        out_specs=(P(AXES, None), P()),
        check_vma=False,
    )
```
